256 devices in a mesh: segment: 2 (over x_lo), tensor: 8 (over y, x_hi), particle: 16 (over z, core).
Axes of the slice: x: 4 (x_hi: 2, x_lo: 2; x = x_hi * 2 + x_lo), y: 4, z: 8, core: 2. Of those that a mesh axis runs over, the one named last changes fastest.
Arguments:
- step_states: bfloat16 [2, 4096, 8192], P('segment', 'particle', 'tensor'), may hold values from -1.5 to 1.5
- norm_gain: float32 [2, 1, 8192], P('segment'), may hold values from 0.1 to 1.9
- w_qkv: bfloat16 [2, 1, 8192, 6144], P('segment', None, 'particle', 'tensor'), may hold values from -0.0625 to 0.0625
- w_out: bfloat16 [2, 1, 8192, 4096], P('segment', None, 'particle', 'tensor'), may hold values from -0.09375 to 0.09375
- prefix_cache: bfloat16 [2, 1, 64, 2, 8, 256, 128], P('segment', None, 'particle', None, 'tensor'), may hold values from -3000 to 3000
- ancestors: int32 [2, 64], P('segment', 'particle'), may hold values from 0 to 63, as said below
- prefix_lengths: int32 [2, 64], P('segment'), may hold values from 32 to 256, as said below
Outputs:
- section_outputs: bfloat16 [2, 4096, 8192], P('segment', 'particle', 'tensor')
The draws below stay inside these ranges and needn't reach their ends.
Inputs may be any that keep to these rules, and one draw needn't show every extreme that they name: `ancestors`: particles form blocks of 4 consecutive ones, 16 blocks on a cycle. A particle's ancestor lies in its own block, the one before or the one after. Every block has a particle descended from the block before and one descended from the block after; at most 3 of a block's particles descend from the block before, at most 3 from the block after, and both bounds are reached in every draw. `prefix_lengths`: in each section some particle's prefix fills all 256 cached positions.
All inputs are finite; a program needn't handle non-finite values.
Results may differ from the reference program's by a relative error of at most 0.015.
The reference program's roundings to bfloat16 on the way count: a program that leaves them out, or rounds other values in their place, can miss the bound.
Values may be sent and summed in bfloat16 or wider, within the bound.
No kernel may reach another device: no remote copies, remote signals or barrier semaphores. Data moves between devices by JAX's collectives and lax.ppermute only.
A program may use at most 128 MiB of HBM per device.

```python
import jax
import jax.numpy as jnp
from jax import lax

D = 8192
HEAD = 128
Q_HEADS = 32
KV_HEADS = 8
LAYERS = 1
PREFIX = 256
PART_DEV = 4
PARTICLES = 64
TOKENS = 4096
QKV_COLS = 6144
ATT_COLS = 4096
N_TENSOR = 8


def draw_ancestors(key, part):
    key = jax.random.fold_in(key, 11)
    split_keys = jax.random.split(key, 5)
    blocks = PARTICLES // PART_DEV
    offsets = jax.random.randint(split_keys[0], (2, blocks, PART_DEV), -1, 2)
    offsets = offsets.at[:, :, 0].set(-1).at[:, :, 1].set(1)
    leftward = jax.random.randint(split_keys[1], (2,), 0, blocks)
    rightward = (leftward + 1 + jax.random.randint(split_keys[2], (2,), 0, blocks - 1)) % blocks
    slot_ids = jnp.arange(PART_DEV, dtype=jnp.int32)
    heavy_left = jnp.where(slot_ids < PART_DEV - 1, -1, 1)
    block_ids = jnp.arange(blocks, dtype=jnp.int32)
    offsets = jnp.where((block_ids[None, :] == leftward[:, None])[:, :, None], heavy_left[None, None, :], offsets)
    offsets = jnp.where((block_ids[None, :] == rightward[:, None])[:, :, None], -heavy_left[None, None, :], offsets)
    scores = jax.random.randint(split_keys[3], (2, blocks, PART_DEV), 0, 1 << 20) * PART_DEV + slot_ids
    shuffle = jnp.argsort(scores, axis=-1, stable=True)
    offsets = jnp.take_along_axis(offsets, shuffle, axis=-1)
    source_rows = jax.random.randint(split_keys[4], (2, blocks, PART_DEV), 0, PART_DEV)
    source_block = (block_ids[None, :, None] + offsets) % blocks
    return (source_block * PART_DEV + source_rows).reshape(2, PARTICLES).astype(jnp.int32)


def draw_prefix_lengths(key, part):
    key = jax.random.fold_in(key, 12)
    split_keys = jax.random.split(key, 2)
    lowest = max(PREFIX // 8, 2)
    drawn = jax.random.randint(split_keys[0], (2, PARTICLES), lowest, PREFIX + 1)
    longest = jax.random.randint(split_keys[1], (2,), 0, PARTICLES)
    drawn = jnp.where(jnp.arange(PARTICLES)[None, :] == longest[:, None], PREFIX, drawn)
    return drawn.astype(jnp.int32)


def draw_prefix_cache(key, part):
    key = jax.random.fold_in(key, 13)
    split_keys = jax.random.split(key, 1)
    full_shape = (2, LAYERS, PARTICLES, 2, KV_HEADS, PREFIX, HEAD)
    combined = jax.random.normal(split_keys[0], full_shape, jnp.float32)
    return combined.astype(jnp.bfloat16)


def levels(own_key, extent, cuts, least, top_value):
    level = 1.0
    for dim, shards_of in cuts:
        heights = jax.random.uniform(jax.random.fold_in(jax.random.fold_in(own_key, 6), dim), (shards_of,), jnp.float32, least / len(cuts), top_value / len(cuts))
        level = level * jnp.repeat(jnp.exp(heights), extent[dim] // shards_of).reshape((-1,) + (1,) * (len(extent) - 1 - dim))
    return level


def centred(key, extent, spread, bound, cuts=(), held_as=jnp.bfloat16):
    array = jax.random.normal(key, extent, jnp.float32) * spread
    if len(cuts) > 0:
        array = levels(key, extent, cuts, -0.22, 0.18) * array
    return jnp.clip(array, min=-bound, max=bound).astype(held_as)


def setup_inputs(seed: int = 0) -> dict:
    key_list = jax.random.split(jax.random.key(seed), 8)
    return {
        "step_states": centred(key_list[0], (2, TOKENS, D), 0.25, 1.5, ((0, 2), (1, 16), (2, 8))),
        "norm_gain": jnp.clip(1.0 + 0.18 * jax.random.normal(key_list[1], (2, LAYERS, D), jnp.float32), 0.1, 1.9),
        "w_qkv": centred(key_list[2], (2, LAYERS, D, QKV_COLS), D ** -0.5, 0.0625, ((0, 2), (2, 16), (3, 8))),
        "w_out": centred(key_list[3], (2, LAYERS, D, ATT_COLS), ATT_COLS ** -0.5, 0.09375, ((0, 2), (2, 16), (3, 8))),
        "prefix_cache": draw_prefix_cache(jax.random.fold_in(key_list[7], 71), 0),
        "ancestors": draw_ancestors(jax.random.fold_in(key_list[7], 71), 0),
        "prefix_lengths": draw_prefix_lengths(jax.random.fold_in(key_list[7], 71), 0),
    }


ROPE_BASE = 1000000.0
NORM_EPSILON = 1e-06

def rotate(values_in, positions):
    half_width = values_in.shape[-1] // 2
    frequency = ROPE_BASE ** (-(jnp.arange(half_width, dtype=jnp.float32) * 2.0 / values_in.shape[-1]))
    angles = positions.astype(jnp.float32)[..., None] * frequency
    cosine_part = jnp.cos(angles)
    sine_part = jnp.sin(angles)
    front_half = values_in[..., :half_width]
    back_half = values_in[..., half_width:]
    return jnp.concatenate([front_half * cosine_part - back_half * sine_part, back_half * cosine_part + front_half * sine_part], -1)

def attend(projected, cache, lengths, group_heads):
    particles = cache.shape[0]
    groups = cache.shape[2]
    prefix = cache.shape[3]
    head_size = cache.shape[4]
    step_tokens = projected.shape[0] // particles
    arranged = projected.reshape(particles, step_tokens, groups, group_heads + 2, head_size)
    positions = lengths[:, None] + jnp.arange(step_tokens, dtype=jnp.int32)[None, :]
    queries = rotate(arranged[:, :, :, :group_heads], positions[:, :, None, None]).astype(jnp.bfloat16)
    keys_new = rotate(arranged[:, :, :, group_heads], positions[:, :, None]).astype(jnp.bfloat16)
    values_new = arranged[:, :, :, group_heads + 1].astype(jnp.bfloat16)
    score_scale = 1.0 / jnp.sqrt(jnp.float32(head_size))
    cache_scores = jnp.einsum('psgih,pglh->pgisl', queries.astype(jnp.float32), cache[:, 0].astype(jnp.float32)) * score_scale
    visible = jnp.arange(prefix, dtype=jnp.int32)[None, :] < lengths[:, None]
    cache_scores = jnp.where(visible[:, None, None, None, :], cache_scores, -1e+30)
    step_scores = jnp.einsum('psgih,ptgh->pgist', queries.astype(jnp.float32), keys_new.astype(jnp.float32)) * score_scale
    causal = jnp.arange(step_tokens)[:, None] >= jnp.arange(step_tokens)[None, :]
    step_scores = jnp.where(causal, step_scores, -1e+30)
    peak = jnp.maximum(lax.optimization_barrier(jnp.max(cache_scores, -1, keepdims=True)), lax.optimization_barrier(jnp.max(step_scores, -1, keepdims=True)))
    cache_weights = jnp.exp(cache_scores - peak)
    step_weights = jnp.exp(step_scores - peak)
    denominator = lax.optimization_barrier(jnp.sum(cache_weights, -1, keepdims=True)) + lax.optimization_barrier(jnp.sum(step_weights, -1, keepdims=True))
    cache_probs = (cache_weights / denominator).astype(jnp.bfloat16)
    step_probs = (step_weights / denominator).astype(jnp.bfloat16)
    attended = jnp.einsum('pgisl,pglh->psgih', cache_probs.astype(jnp.float32), cache[:, 1].astype(jnp.float32))
    attended = attended + jnp.einsum('pgist,ptgh->psgih', step_probs.astype(jnp.float32), values_new.astype(jnp.float32))
    return attended.astype(jnp.bfloat16).reshape(particles * step_tokens, groups * group_heads * head_size)

def section(states, gains, qkv_weights, out_weights, cache, parents, length_table):
    lengths = length_table[parents].astype(jnp.int32)
    picked = cache[:, parents]
    group_heads = Q_HEADS // KV_HEADS
    hidden = states
    for layer_index in range(LAYERS):
        full_rows = hidden.astype(jnp.float32)
        normed = (full_rows * lax.rsqrt(lax.optimization_barrier(jnp.mean(full_rows * full_rows, -1, keepdims=True)) + NORM_EPSILON) * gains[layer_index]).astype(jnp.bfloat16)
        projected = jnp.dot(normed, qkv_weights[layer_index], preferred_element_type=jnp.float32)
        attended = attend(projected, picked[layer_index], lengths, group_heads)
        group_cols = attended.shape[1] // N_TENSOR
        summed = jnp.zeros(full_rows.shape, jnp.float32)
        for tensor_index in range(N_TENSOR):
            lower_col = tensor_index * group_cols
            partial_term = jnp.dot(attended[:, lower_col:lower_col + group_cols], out_weights[layer_index][:, lower_col:lower_col + group_cols].T, preferred_element_type=jnp.float32)
            summed = summed + lax.optimization_barrier(partial_term.astype(jnp.bfloat16)).astype(jnp.float32)
        hidden = (full_rows + summed).astype(jnp.bfloat16)
    return hidden

def reference(step_states, norm_gain, w_qkv, w_out, prefix_cache, ancestors, prefix_lengths):
    section_one = section(step_states[0], norm_gain[0], w_qkv[0], w_out[0], prefix_cache[0], ancestors[0], prefix_lengths[0])
    section_two = section(step_states[1], norm_gain[1], w_qkv[1], w_out[1], prefix_cache[1], ancestors[1], prefix_lengths[1])
    return jnp.stack([section_two, section_one])
```

```python
import jax
import jax.numpy as jnp
from jax import lax
from jax.sharding import PartitionSpec as P

Q_HEADS = 32
KV_HEADS = 8

ROPE_BASE = 1000000.0
NORM_EPSILON = 1e-06

AXES = ("segment", "tensor", "particle")
SEG, NY, NXH, NZ, NC = 2, 4, 2, 8, 2


def moves(ds=0, dy=0, dxh=0, dz=0, dc=0):
    pairs = []
    for s in range(SEG):
        for y in range(NY):
            for xh in range(NXH):
                for z in range(NZ):
                    for c in range(NC):
                        src = ((s * NY + y) * NXH + xh) * NZ * NC + z * NC + c
                        to = (
                            ((s + ds) % SEG * NY + (y + dy) % NY) * NXH + (xh + dxh) % NXH
                        ) * NZ * NC + (z + dz) % NZ * NC + (c + dc) % NC
                        pairs.append((src, to))
    return pairs


def send(value, **shift):
    return lax.ppermute(value, AXES, moves(**shift))


def rotate(values_in, positions):
    half_width = values_in.shape[-1] // 2
    frequency = ROPE_BASE ** (
        -(jnp.arange(half_width, dtype=jnp.float32) * 2.0 / values_in.shape[-1])
    )
    angles = positions.astype(jnp.float32)[..., None] * frequency
    cosine_part = jnp.cos(angles)
    sine_part = jnp.sin(angles)
    front_half = values_in[..., :half_width]
    back_half = values_in[..., half_width:]
    return jnp.concatenate(
        [
            front_half * cosine_part - back_half * sine_part,
            back_half * cosine_part + front_half * sine_part,
        ],
        -1,
    )


def attend(projected, cache, lengths, group_heads):
    particles = cache.shape[0]
    groups = cache.shape[2]
    prefix = cache.shape[3]
    head_size = cache.shape[4]
    step_tokens = projected.shape[0] // particles
    arranged = projected.reshape(particles, step_tokens, groups, group_heads + 2, head_size)
    positions = lengths[:, None] + jnp.arange(step_tokens, dtype=jnp.int32)[None, :]
    queries = rotate(arranged[:, :, :, :group_heads], positions[:, :, None, None]).astype(
        jnp.bfloat16
    )
    keys_new = rotate(arranged[:, :, :, group_heads], positions[:, :, None]).astype(jnp.bfloat16)
    values_new = arranged[:, :, :, group_heads + 1].astype(jnp.bfloat16)
    score_scale = 1.0 / jnp.sqrt(jnp.float32(head_size))
    cache_scores = (
        jnp.einsum("psgih,pglh->pgisl", queries, cache[:, 0], preferred_element_type=jnp.float32)
        * score_scale
    )
    visible = jnp.arange(prefix, dtype=jnp.int32)[None, :] < lengths[:, None]
    cache_scores = jnp.where(visible[:, None, None, None, :], cache_scores, -1e30)
    step_scores = (
        jnp.einsum("psgih,ptgh->pgist", queries, keys_new, preferred_element_type=jnp.float32)
        * score_scale
    )
    causal = jnp.arange(step_tokens)[:, None] >= jnp.arange(step_tokens)[None, :]
    step_scores = jnp.where(causal, step_scores, -1e30)
    peak = jnp.maximum(
        jnp.max(cache_scores, -1, keepdims=True), jnp.max(step_scores, -1, keepdims=True)
    )
    cache_weights = jnp.exp(cache_scores - peak)
    step_weights = jnp.exp(step_scores - peak)
    denominator = jnp.sum(cache_weights, -1, keepdims=True) + jnp.sum(
        step_weights, -1, keepdims=True
    )
    cache_probs = (cache_weights / denominator).astype(jnp.bfloat16)
    step_probs = (step_weights / denominator).astype(jnp.bfloat16)
    attended = jnp.einsum(
        "pgisl,pglh->psgih", cache_probs, cache[:, 1], preferred_element_type=jnp.float32
    )
    attended = attended + jnp.einsum(
        "pgist,ptgh->psgih", step_probs, values_new, preferred_element_type=jnp.float32
    )
    return attended.astype(jnp.bfloat16).reshape(
        particles * step_tokens, groups * group_heads * head_size
    )


def one_hot(chosen, columns):
    return (chosen[:, None] == jnp.arange(columns, dtype=jnp.int32)[None, :]).astype(jnp.bfloat16)


def pick_rows(selector, source):
    flattened = source.reshape(source.shape[0], source.shape[1], -1)
    selected = jnp.einsum("jk,lkr->ljr", selector, flattened, preferred_element_type=jnp.float32)
    return selected.astype(jnp.bfloat16).reshape(
        (source.shape[0], selector.shape[0]) + source.shape[2:]
    )


def picked_cache(prefix_cache, ancestors, prefix_lengths):
    devices = lax.axis_size("particle")
    own_index = lax.axis_index("particle")
    per_device = ancestors.shape[1]
    parents = ancestors[0]
    length_table = prefix_lengths[0]
    lengths = jnp.sum(
        jnp.where(
            parents[:, None] == jnp.arange(length_table.shape[0], dtype=jnp.int32)[None, :],
            length_table[None, :],
            0,
        ),
        axis=1,
    )
    distance = (parents // per_device - own_index) % devices
    offset = jnp.where(distance == 0, 0, jnp.where(distance == 1, 1, -1))
    source_row = parents % per_device
    caches = prefix_cache[0]
    before = lax.ppermute(caches, "particle", [(i, (i + 1) % devices) for i in range(devices)])
    after = lax.ppermute(caches, "particle", [((i + 1) % devices, i) for i in range(devices)])
    extended = jnp.concatenate([before, caches, after], axis=1)
    picked = pick_rows(one_hot((offset + 1) * per_device + source_row, 3 * per_device), extended)
    return picked[0], lengths


def ring(shard, after=None):
    rows = shard.shape[0] // 2
    out = [[], []]
    for half in range(2):
        part = shard[half * rows : (half + 1) * rows]
        out[half].append((0, part))
    flow = {(half, d): out[half][0][1] for half in range(2) for d in (1, -1)}
    for step in range(1, NZ // 2 + 1):
        for half in range(2):
            for d in (1, -1):
                if step == NZ // 2 and d != (1, -1)[half]:
                    continue
                flow[half, d] = send(flow[half, d], dz=d)
                out[half].append((-d * step, flow[half, d]))
    return out


def swapped(own_first):
    half = own_first.shape[0] // 2
    return own_first[half:], own_first[:half]


def body(step_states, norm_gain, w_qkv, w_out, prefix_cache, ancestors, prefix_lengths):
    t = lax.axis_index("tensor")
    y, xh = t // NXH, t % NXH
    z, c = lax.axis_index("particle") // NC, lax.axis_index("particle") % NC
    group_heads = Q_HEADS // KV_HEADS
    x0 = step_states[0]
    tokens, features = x0.shape
    half_f = features // NC

    picked, lengths = picked_cache(prefix_cache, ancestors, prefix_lengths)

    mine = lax.dynamic_slice_in_dim(x0, c * half_f, half_f, axis=1)
    other = lax.dynamic_slice_in_dim(x0, (1 - c) * half_f, half_f, axis=1)
    xc = jnp.concatenate([mine, send(other, dc=1)], axis=0)

    pair = jnp.stack([xc, send(xc, dxh=1)])
    from_before = send(pair, dy=1)
    from_after = send(pair, dy=-1)
    far_a = send(from_before[0], dy=1)
    far_b = send(from_after[1], dy=-1)
    xg = jnp.concatenate([pair, from_after, jnp.stack([far_a, far_b]), from_before], axis=0)

    qkv_parts = ring(w_qkv[0, 0])

    xf = xg.astype(jnp.float32)
    squares = jnp.sum(xf * xf, axis=(0, 2))
    partner_squares = send(squares, dc=1)
    squares = squares + jnp.concatenate(swapped(partner_squares))
    scale = lax.rsqrt(squares / (features * NY * NXH) + NORM_EPSILON)
    gains = norm_gain[0, 0].reshape(NY, NXH, NC, half_f)
    gains = lax.dynamic_index_in_dim(gains, c, axis=2, keepdims=False)
    gains = jnp.take(gains, (y + jnp.arange(NY)) % NY, axis=0)
    gains = jnp.where(xh == 0, gains, gains[:, ::-1]).reshape(NY * NXH, 1, half_f)
    normed = (xf * scale[None, :, None] * gains).astype(jnp.bfloat16)

    def feature_block(zz):
        return ((zz // NXH - y) % NY) * NXH + (zz % NXH + xh) % NXH

    total = jnp.zeros((2 * tokens, w_qkv.shape[3]), jnp.float32)
    rows = w_qkv.shape[2] // 2
    for k in range(NZ):
        for half in range(2):
            offset, part = qkv_parts[half][k]
            zz = (z + offset) % NZ
            block = lax.dynamic_slice(
                normed, (feature_block(zz), 0, half * rows), (1, 2 * tokens, rows)
            )[0]
            total = total + jnp.dot(block, part, preferred_element_type=jnp.float32)
    own, partners = total[:tokens], total[tokens:]
    projected = own + send(partners, dc=1)

    attended = attend(projected, picked, lengths, group_heads)
    attended = jnp.concatenate([attended, send(attended, dc=1)], axis=0)

    first, w_late = lax.optimization_barrier((qkv_parts[0][-2][1], w_out[0, 0]))
    out_parts = ring(w_late)
    chunk = w_out.shape[2] // 2
    results = []
    for half in range(2):
        terms = jnp.zeros((NZ, 2 * tokens, chunk), jnp.bfloat16)
        for offset, part in out_parts[half]:
            term = lax.dot_general(
                attended, part, (((1,), (1,)), ((), ())), preferred_element_type=jnp.float32
            ).astype(jnp.bfloat16)
            terms = lax.dynamic_update_slice(terms, term[None], ((z + offset) % NZ, 0, 0))
        terms = terms.reshape(NY, NXH, 2 * tokens, chunk)
        at = lambda dy: lax.dynamic_index_in_dim(terms, (y + dy) % NY, axis=0, keepdims=False)
        summed = at(0).astype(jnp.float32)
        for dy in (1, -1, 2):
            summed = summed + send(at(dy), dy=dy).astype(jnp.float32)
        keep = lax.dynamic_index_in_dim(summed, xh, axis=0, keepdims=False)
        give = lax.dynamic_index_in_dim(summed, 1 - xh, axis=0, keepdims=False)
        keep = keep + send(give.astype(jnp.bfloat16), dxh=1).astype(jnp.float32)
        hidden = xc[:, half * chunk : (half + 1) * chunk].astype(jnp.float32)
        hidden = (hidden + keep).astype(jnp.bfloat16)
        same = send(hidden[:tokens], ds=1)
        cross = send(hidden[tokens:], ds=1, dc=1)
        results.append((same, cross))
    same = jnp.concatenate([r[0] for r in results], axis=1)
    cross = jnp.concatenate([r[1] for r in results], axis=1)
    low = jnp.where(c == 0, same, cross)
    high = jnp.where(c == 0, cross, same)
    return jnp.concatenate([low, high], axis=1)[None]


def solution(mesh):
    placed = (
        P("segment", "particle", "tensor"),
        P("segment", None, None),
        P("segment", None, "particle", "tensor"),
        P("segment", None, "particle", "tensor"),
        P("segment", None, "particle", None, "tensor", None, None),
        P("segment", "particle"),
        P("segment", None),
    )
    return jax.shard_map(
        body,
        mesh=mesh,
        in_specs=placed,
        out_specs=P("segment", "particle", "tensor"),
        check_vma=False,
    )
```

```python
import jax
import jax.numpy as jnp
from jax import lax
from jax.experimental import pallas as pl
from jax.experimental.pallas import tpu as pltpu
from jax.sharding import PartitionSpec as P

Q_HEADS = 32
KV_HEADS = 8

ROPE_BASE = 1000000.0
NORM_EPSILON = 1e-06

AXES = ("segment", "tensor", "particle")
SEG, NY, NXH, NZ, NC = 2, 4, 2, 8, 2
SCOPE = pltpu.CompilerParams(vmem_limit_bytes=40 * 2**20)


def moves(ds=0, dy=0, dxh=0, dz=0, dc=0):
    pairs = []
    for s in range(SEG):
        for y in range(NY):
            for xh in range(NXH):
                for z in range(NZ):
                    for c in range(NC):
                        src = ((s * NY + y) * NXH + xh) * NZ * NC + z * NC + c
                        to = (
                            ((s + ds) % SEG * NY + (y + dy) % NY) * NXH + (xh + dxh) % NXH
                        ) * NZ * NC + (z + dz) % NZ * NC + (c + dc) % NC
                        pairs.append((src, to))
    return pairs


def send(value, **shift):
    return lax.ppermute(value, AXES, moves(**shift))


def rotation(lengths, step_tokens, head_size):
    half_width = head_size // 2
    frequency = ROPE_BASE ** (
        -(jnp.arange(half_width, dtype=jnp.float32) * 2.0 / head_size)
    )
    positions = lengths[:, None] + jnp.arange(step_tokens, dtype=jnp.int32)[None, :]
    angles = positions.reshape(-1).astype(jnp.float32)[:, None] * frequency
    cosine_part = jnp.cos(angles)
    sine_part = jnp.sin(angles)
    return (
        jnp.concatenate([cosine_part, cosine_part], axis=1),
        jnp.concatenate([-sine_part, sine_part], axis=1),
    )


def attend_kernel(group_heads, lengths_ref, x_ref, cos_ref, sin_ref, cache_ref, o_ref):
    particles, _, prefix, head = cache_ref.shape
    steps = x_ref.shape[0] // particles
    score_scale = 1.0 / jnp.sqrt(jnp.float32(head))
    across = (((1,), (1,)), ((), ()))
    for p in range(particles):
        mine = pl.ds(p * steps, steps)
        cosine_part, sine_part = cos_ref[mine, :], sin_ref[mine, :]

        def rotated(k):
            v = x_ref[mine, k * head : (k + 1) * head]
            return v * cosine_part + pltpu.roll(v, head // 2, 1) * sine_part

        queries = jnp.concatenate([rotated(k) for k in range(group_heads)], axis=0)
        queries = queries.astype(jnp.bfloat16)
        keys_new = rotated(group_heads).astype(jnp.bfloat16)
        values_new = x_ref[mine, (group_heads + 1) * head :].astype(jnp.bfloat16)
        cache_scores = (
            lax.dot_general(queries, cache_ref[p, 0], across, preferred_element_type=jnp.float32)
            * score_scale
        )
        spots = lax.broadcasted_iota(jnp.int32, cache_scores.shape, 1)
        cache_scores = jnp.where(spots < lengths_ref[p], cache_scores, -1e30)
        step_scores = (
            lax.dot_general(queries, keys_new, across, preferred_element_type=jnp.float32)
            * score_scale
        )
        token = lax.rem(lax.broadcasted_iota(jnp.int32, step_scores.shape, 0), steps)
        other = lax.broadcasted_iota(jnp.int32, step_scores.shape, 1)
        step_scores = jnp.where(token >= other, step_scores, -1e30)
        peak = jnp.maximum(
            jnp.max(cache_scores, -1, keepdims=True), jnp.max(step_scores, -1, keepdims=True)
        )
        cache_weights = jnp.exp(cache_scores - peak)
        step_weights = jnp.exp(step_scores - peak)
        share = 1.0 / (
            jnp.sum(cache_weights, -1, keepdims=True) + jnp.sum(step_weights, -1, keepdims=True)
        )
        attended = jnp.dot(
            (cache_weights * share).astype(jnp.bfloat16),
            cache_ref[p, 1],
            preferred_element_type=jnp.float32,
        ) + jnp.dot(
            (step_weights * share).astype(jnp.bfloat16),
            values_new,
            preferred_element_type=jnp.float32,
        )
        attended = attended.astype(jnp.bfloat16)
        for k in range(group_heads):
            o_ref[mine, k * head : (k + 1) * head] = attended[k * steps : (k + 1) * steps]


def attend(projected, cosine_part, sine_part, cache, lengths, group_heads):
    head = cache.shape[-1]
    whole = pl.BlockSpec(memory_space=pltpu.VMEM)
    return pl.pallas_call(
        lambda *refs: attend_kernel(group_heads, *refs),
        in_specs=[pl.BlockSpec(memory_space=pltpu.SMEM)] + [whole] * 4,
        out_specs=whole,
        out_shape=jax.ShapeDtypeStruct((projected.shape[0], group_heads * head), jnp.bfloat16),
        compiler_params=SCOPE,
        cost_estimate=pl.CostEstimate(
            flops=4 * projected.shape[0] * group_heads * head * (cache.shape[2] + 64),
            bytes_accessed=2 * cache.size + 4 * projected.size,
            transcendentals=0,
        ),
    )(lengths, projected, cosine_part, sine_part, cache)


def one_hot(chosen, columns):
    return (chosen[:, None] == jnp.arange(columns, dtype=jnp.int32)[None, :]).astype(jnp.bfloat16)


def pick_rows(selector, source):
    flattened = source.reshape(source.shape[0], source.shape[1], -1)
    selected = jnp.einsum("jk,lkr->ljr", selector, flattened, preferred_element_type=jnp.float32)
    return selected.astype(jnp.bfloat16).reshape(
        (source.shape[0], selector.shape[0]) + source.shape[2:]
    )


def picked_cache(prefix_cache, ancestors, prefix_lengths):
    devices = lax.axis_size("particle")
    own_index = lax.axis_index("particle")
    per_device = ancestors.shape[1]
    parents = ancestors[0]
    length_table = prefix_lengths[0]
    lengths = jnp.sum(
        jnp.where(
            parents[:, None] == jnp.arange(length_table.shape[0], dtype=jnp.int32)[None, :],
            length_table[None, :],
            0,
        ),
        axis=1,
    )
    distance = (parents // per_device - own_index) % devices
    offset = jnp.where(distance == 0, 0, jnp.where(distance == 1, 1, -1))
    source_row = parents % per_device
    caches = prefix_cache[0]
    before = lax.ppermute(caches, "particle", [(i, (i + 1) % devices) for i in range(devices)])
    after = lax.ppermute(caches, "particle", [((i + 1) % devices, i) for i in range(devices)])
    extended = jnp.concatenate([before, caches, after], axis=1)
    picked = pick_rows(one_hot((offset + 1) * per_device + source_row, 3 * per_device), extended)
    return picked[0], lengths


def ring(block):
    half = block.shape[0] // 2
    found = {0: block}
    flow = {1: block, -1: block}
    for step in range(1, NZ // 2):
        for d in (1, -1):
            flow[d] = send(flow[d], dz=d)
            found[-d * step % NZ] = flow[d]
    far_low = send(flow[1][:half], dz=1)
    far_high = send(flow[-1][half:], dz=-1)
    found[NZ // 2] = jnp.concatenate([far_low, far_high], axis=0)
    return found


def term(a, w):
    return lax.dot_general(
        a, w, (((1,), (1,)), ((), ())), preferred_element_type=jnp.float32
    ).astype(jnp.bfloat16)


def terms_kernel(a_ref, w_ref, o_ref):
    o_ref[0] = term(a_ref[...], w_ref[...])


def head_terms(a, w):
    shards = NY * NXH
    rows = w.shape[0] // shards
    return pl.pallas_call(
        terms_kernel,
        grid=(shards,),
        in_specs=[
            pl.BlockSpec(a.shape, lambda k: (0, 0)),
            pl.BlockSpec((rows, w.shape[1]), lambda k: (k, 0)),
        ],
        out_specs=pl.BlockSpec((1, a.shape[0], rows), lambda k: (k, 0, 0)),
        out_shape=jax.ShapeDtypeStruct((shards, a.shape[0], rows), jnp.bfloat16),
        compiler_params=SCOPE,
        cost_estimate=pl.CostEstimate(
            flops=2 * a.size * w.shape[0],
            bytes_accessed=2 * (a.size + w.size + a.shape[0] * w.shape[0]),
            transcendentals=0,
        ),
    )(a, w)


def ring_terms_kernel(order, place_ref, a_ref, *refs):
    own, partners, o_ref = refs[: len(order)], refs[len(order) : -1], refs[-1]
    z, c = place_ref[0], place_ref[1]
    rows = own[0].shape[0]
    a = a_ref[...]
    at = 0
    for k, block in zip(order, own):
        to = lax.rem(z + k, NZ)
        o_ref[to, :, pl.ds(pl.multiple_of(c * rows, rows), rows)] = term(a, block[...])
    for group in partners:
        for g in range(group.shape[0]):
            to = lax.rem(z + order[at], NZ)
            o_ref[to, :, pl.ds(pl.multiple_of((1 - c) * rows, rows), rows)] = term(a, group[g])
            at += 1


def ring_terms(a, order, own, partners, place):
    rows = own[0].shape[0]
    whole = pl.BlockSpec(memory_space=pltpu.VMEM)
    return pl.pallas_call(
        lambda *refs: ring_terms_kernel(order, *refs),
        in_specs=[pl.BlockSpec(memory_space=pltpu.SMEM)]
        + [whole] * (1 + len(own) + len(partners)),
        out_specs=whole,
        out_shape=jax.ShapeDtypeStruct((NZ, a.shape[0], NC * rows), jnp.bfloat16),
        compiler_params=SCOPE,
        cost_estimate=pl.CostEstimate(
            flops=2 * a.size * NZ * NC * rows,
            bytes_accessed=2 * (a.size + NZ * NC * rows * (a.shape[0] + a.shape[1])),
            transcendentals=0,
        ),
    )(place, a, *own, *partners)


def body(step_states, norm_gain, w_qkv, w_out, prefix_cache, ancestors, prefix_lengths):
    t = lax.axis_index("tensor")
    y, xh = t // NXH, t % NXH
    z, c = lax.axis_index("particle") // NC, lax.axis_index("particle") % NC
    group_heads = Q_HEADS // KV_HEADS
    x0 = step_states[0]
    tokens, features = x0.shape
    shards = NY * NXH
    rows = w_out.shape[2] // 2

    w_full = lax.all_gather(w_qkv[0, 0], "particle", axis=0, tiled=True)

    pair = jnp.stack([x0, send(x0, dxh=1)])
    from_before = send(pair, dy=1)
    from_after = send(pair, dy=-1)
    far_a = send(from_before[0], dy=1)
    far_b = send(from_after[1], dy=-1)
    found = jnp.concatenate([pair, from_after, jnp.stack([far_a, far_b]), from_before], axis=0)
    blocks = [
        lax.dynamic_index_in_dim(
            found, ((k // NXH - y) % NY) * NXH + (k + xh) % NXH, axis=0, keepdims=False
        )
        for k in range(shards)
    ]
    full_rows = jnp.concatenate(blocks, axis=1).astype(jnp.float32)
    normed = (
        full_rows
        * lax.rsqrt(jnp.mean(full_rows * full_rows, -1, keepdims=True) + NORM_EPSILON)
        * norm_gain[0, 0]
    ).astype(jnp.bfloat16)

    hidden = send(x0, ds=1)
    picked, lengths = picked_cache(prefix_cache, ancestors, prefix_lengths)

    around = ring(w_out[0, 0, :rows])
    order = (0, 1, 7, 2, 6, 3, 5, 4)
    own = [around[k] for k in order]
    partners = [send(jnp.stack(own[:5]), dc=1), send(jnp.stack(own[5:]), dc=1)]

    cosine_part, sine_part = rotation(lengths, tokens // ancestors.shape[1], picked.shape[-1])
    cache = picked.reshape(picked.shape[0], 2, picked.shape[3], picked.shape[4])
    w_full, normed, cache, cosine_part, sine_part, hidden, own, partners = lax.optimization_barrier(
        (w_full, normed, cache, cosine_part, sine_part, hidden, own, partners)
    )
    second = lax.all_gather(w_out[0, 0, rows:], "particle", axis=0, tiled=True)
    projected = jnp.dot(normed, w_full, preferred_element_type=jnp.float32)
    attended = attend(projected, cosine_part, sine_part, cache, lengths, group_heads)

    results = []
    for half in range(2):
        if half == 0:
            terms = ring_terms(attended, order, own, partners, jnp.stack([z, c]))
        else:
            terms = head_terms(attended, second)
        terms = terms.reshape(NY, NXH, tokens, NC * rows)
        mid = tokens // 2

        def low_high(dy):
            block = lax.dynamic_index_in_dim(terms, (y + dy) % NY, axis=0, keepdims=False)
            return block[:, :mid], block[:, mid:]

        far_up, far_down = low_high(2)
        far_up, far_down = send(far_up, dy=1), send(far_down, dy=-1)
        up_low, up_high = low_high(1)
        down_low, down_high = low_high(-1)
        direct_up, direct_down = send(up_high, dy=1), send(down_low, dy=-1)
        relayed_up = send(
            (up_low.astype(jnp.float32) + far_up.astype(jnp.float32)).astype(jnp.bfloat16), dy=1
        )
        relayed_down = send(
            (down_high.astype(jnp.float32) + far_down.astype(jnp.float32)).astype(jnp.bfloat16),
            dy=-1,
        )
        here_low, here_high = low_high(0)
        low = (
            here_low.astype(jnp.float32)
            + relayed_up.astype(jnp.float32)
            + direct_down.astype(jnp.float32)
        )
        high = (
            here_high.astype(jnp.float32)
            + relayed_down.astype(jnp.float32)
            + direct_up.astype(jnp.float32)
        )
        summed = jnp.concatenate([low, high], axis=1).astype(jnp.bfloat16)
        attended, summed = lax.optimization_barrier((attended, summed))
        same = send(jnp.where(xh == 0, summed[0], summed[1]), ds=1)
        cross = send(jnp.where(xh == 0, summed[1], summed[0]), ds=1, dxh=1)
        results.append(same.astype(jnp.float32) + cross.astype(jnp.float32))
    summed = jnp.concatenate(
        [r[:, k * rows : (k + 1) * rows] for k in range(NC) for r in results], axis=1
    )
    return (hidden.astype(jnp.float32) + summed).astype(jnp.bfloat16)[None]


def solution(mesh):
    placed = (
        P("segment", "particle", "tensor"),
        P("segment", None, None),
        P("segment", None, "particle", "tensor"),
        P("segment", None, "particle", "tensor"),
        P("segment", None, "particle", None, "tensor", None, None),
        P("segment", "particle"),
        P("segment", None),
    )
    return jax.shard_map(
        body,
        mesh=mesh,
        in_specs=placed,
        out_specs=P("segment", "particle", "tensor"),
        check_vma=False,
    )
```

```python
import jax
import jax.numpy as jnp
from jax import lax
from jax.experimental import pallas as pl
from jax.experimental.pallas import tpu as pltpu
from jax.sharding import PartitionSpec as P

Q_HEADS = 32
KV_HEADS = 8

ROPE_BASE = 1000000.0
NORM_EPSILON = 1e-06

AXES = ("segment", "tensor", "particle")
SEG, NY, NXH, NZ, NC = 2, 4, 2, 8, 2
SCOPE = pltpu.CompilerParams(vmem_limit_bytes=40 * 2**20)


def moves(ds=0, dy=0, dxh=0, dz=0, dc=0):
    pairs = []
    for s in range(SEG):
        for y in range(NY):
            for xh in range(NXH):
                for z in range(NZ):
                    for c in range(NC):
                        src = ((s * NY + y) * NXH + xh) * NZ * NC + z * NC + c
                        to = (
                            ((s + ds) % SEG * NY + (y + dy) % NY) * NXH + (xh + dxh) % NXH
                        ) * NZ * NC + (z + dz) % NZ * NC + (c + dc) % NC
                        pairs.append((src, to))
    return pairs


def send(value, **shift):
    return lax.ppermute(value, AXES, moves(**shift))


def rotation(lengths, step_tokens, head_size):
    half_width = head_size // 2
    frequency = ROPE_BASE ** (
        -(jnp.arange(half_width, dtype=jnp.float32) * 2.0 / head_size)
    )
    positions = lengths[:, None] + jnp.arange(step_tokens, dtype=jnp.int32)[None, :]
    angles = positions.reshape(-1).astype(jnp.float32)[:, None] * frequency
    cosine_part = jnp.cos(angles)
    sine_part = jnp.sin(angles)
    return (
        jnp.concatenate([cosine_part, cosine_part], axis=1),
        jnp.concatenate([-sine_part, sine_part], axis=1),
    )


def attend_kernel(group_heads, lengths_ref, x_ref, cos_ref, sin_ref, cache_ref, o_ref):
    particles, _, prefix, head = cache_ref.shape
    steps = x_ref.shape[0] // particles
    score_scale = 1.0 / jnp.sqrt(jnp.float32(head))
    across = (((1,), (1,)), ((), ()))
    for p in range(particles):
        mine = pl.ds(p * steps, steps)
        cosine_part, sine_part = cos_ref[mine, :], sin_ref[mine, :]

        def rotated(k):
            v = x_ref[mine, k * head : (k + 1) * head]
            return v * cosine_part + pltpu.roll(v, head // 2, 1) * sine_part

        queries = jnp.concatenate([rotated(k) for k in range(group_heads)], axis=0)
        queries = queries.astype(jnp.bfloat16)
        keys_new = rotated(group_heads).astype(jnp.bfloat16)
        values_new = x_ref[mine, (group_heads + 1) * head :].astype(jnp.bfloat16)
        cache_scores = (
            lax.dot_general(queries, cache_ref[p, 0], across, preferred_element_type=jnp.float32)
            * score_scale
        )
        spots = lax.broadcasted_iota(jnp.int32, cache_scores.shape, 1)
        cache_scores = jnp.where(spots < lengths_ref[p], cache_scores, -1e30)
        step_scores = (
            lax.dot_general(queries, keys_new, across, preferred_element_type=jnp.float32)
            * score_scale
        )
        token = lax.rem(lax.broadcasted_iota(jnp.int32, step_scores.shape, 0), steps)
        other = lax.broadcasted_iota(jnp.int32, step_scores.shape, 1)
        step_scores = jnp.where(token >= other, step_scores, -1e30)
        peak = jnp.maximum(
            jnp.max(cache_scores, -1, keepdims=True), jnp.max(step_scores, -1, keepdims=True)
        )
        cache_weights = jnp.exp(cache_scores - peak)
        step_weights = jnp.exp(step_scores - peak)
        share = 1.0 / (
            jnp.sum(cache_weights, -1, keepdims=True) + jnp.sum(step_weights, -1, keepdims=True)
        )
        attended = jnp.dot(
            (cache_weights * share).astype(jnp.bfloat16),
            cache_ref[p, 1],
            preferred_element_type=jnp.float32,
        ) + jnp.dot(
            (step_weights * share).astype(jnp.bfloat16),
            values_new,
            preferred_element_type=jnp.float32,
        )
        attended = attended.astype(jnp.bfloat16)
        for k in range(group_heads):
            o_ref[mine, k * head : (k + 1) * head] = attended[k * steps : (k + 1) * steps]


def attend(projected, cosine_part, sine_part, cache, lengths, group_heads):
    head = cache.shape[-1]
    whole = pl.BlockSpec(memory_space=pltpu.VMEM)
    return pl.pallas_call(
        lambda *refs: attend_kernel(group_heads, *refs),
        in_specs=[pl.BlockSpec(memory_space=pltpu.SMEM)] + [whole] * 4,
        out_specs=whole,
        out_shape=jax.ShapeDtypeStruct((projected.shape[0], group_heads * head), jnp.bfloat16),
        compiler_params=SCOPE,
        cost_estimate=pl.CostEstimate(
            flops=4 * projected.shape[0] * group_heads * head * (cache.shape[2] + 64),
            bytes_accessed=2 * cache.size + 4 * projected.size,
            transcendentals=0,
        ),
    )(lengths, projected, cosine_part, sine_part, cache)


def one_hot(chosen, columns):
    return (chosen[:, None] == jnp.arange(columns, dtype=jnp.int32)[None, :]).astype(jnp.bfloat16)


def pick_rows(selector, source):
    flattened = source.reshape(source.shape[0], source.shape[1], -1)
    selected = jnp.einsum("jk,lkr->ljr", selector, flattened, preferred_element_type=jnp.float32)
    return selected.astype(jnp.bfloat16).reshape(
        (source.shape[0], selector.shape[0]) + source.shape[2:]
    )


def picked_cache(prefix_cache, ancestors, prefix_lengths):
    devices = lax.axis_size("particle")
    own_index = lax.axis_index("particle")
    per_device = ancestors.shape[1]
    parents = ancestors[0]
    length_table = prefix_lengths[0]
    lengths = jnp.sum(
        jnp.where(
            parents[:, None] == jnp.arange(length_table.shape[0], dtype=jnp.int32)[None, :],
            length_table[None, :],
            0,
        ),
        axis=1,
    )
    distance = (parents // per_device - own_index) % devices
    offset = jnp.where(distance == 0, 0, jnp.where(distance == 1, 1, -1))
    source_row = parents % per_device
    caches = prefix_cache[0]
    before = lax.ppermute(caches, "particle", [(i, (i + 1) % devices) for i in range(devices)])
    after = lax.ppermute(caches, "particle", [((i + 1) % devices, i) for i in range(devices)])
    extended = jnp.concatenate([before, caches, after], axis=1)
    picked = pick_rows(one_hot((offset + 1) * per_device + source_row, 3 * per_device), extended)
    return picked[0], lengths


def ring(block):
    half = block.shape[0] // 2
    found = {0: block}
    flow = {1: block, -1: block}
    for step in range(1, NZ // 2):
        for d in (1, -1):
            flow[d] = send(flow[d], dz=d)
            found[-d * step % NZ] = flow[d]
    far_low = send(flow[1][:half], dz=1)
    far_high = send(flow[-1][half:], dz=-1)
    found[NZ // 2] = jnp.concatenate([far_low, far_high], axis=0)
    return found


def term(a, w):
    return lax.dot_general(
        a, w, (((1,), (1,)), ((), ())), preferred_element_type=jnp.float32
    ).astype(jnp.bfloat16)


def terms_kernel(a_ref, w_ref, o_ref):
    o_ref[0] = term(a_ref[...], w_ref[...])


def head_terms(a, w):
    shards = NY * NXH
    rows = w.shape[0] // shards
    return pl.pallas_call(
        terms_kernel,
        grid=(shards,),
        in_specs=[
            pl.BlockSpec(a.shape, lambda k: (0, 0)),
            pl.BlockSpec((rows, w.shape[1]), lambda k: (k, 0)),
        ],
        out_specs=pl.BlockSpec((1, a.shape[0], rows), lambda k: (k, 0, 0)),
        out_shape=jax.ShapeDtypeStruct((shards, a.shape[0], rows), jnp.bfloat16),
        compiler_params=SCOPE,
        cost_estimate=pl.CostEstimate(
            flops=2 * a.size * w.shape[0],
            bytes_accessed=2 * (a.size + w.size + a.shape[0] * w.shape[0]),
            transcendentals=0,
        ),
    )(a, w)


def ring_terms_kernel(order, place_ref, a_ref, *refs):
    own, partners, o_ref = refs[: len(order)], refs[len(order) : -1], refs[-1]
    z, c = place_ref[0], place_ref[1]
    rows = own[0].shape[0]
    a = a_ref[...]
    at = 0
    for k, block in zip(order, own):
        to = lax.rem(z + k, NZ)
        o_ref[to, :, pl.ds(pl.multiple_of(c * rows, rows), rows)] = term(a, block[...])
    for group in partners:
        for g in range(group.shape[0]):
            to = lax.rem(z + order[at], NZ)
            o_ref[to, :, pl.ds(pl.multiple_of((1 - c) * rows, rows), rows)] = term(a, group[g])
            at += 1


def ring_terms(a, order, own, partners, place):
    rows = own[0].shape[0]
    whole = pl.BlockSpec(memory_space=pltpu.VMEM)
    return pl.pallas_call(
        lambda *refs: ring_terms_kernel(order, *refs),
        in_specs=[pl.BlockSpec(memory_space=pltpu.SMEM)]
        + [whole] * (1 + len(own) + len(partners)),
        out_specs=whole,
        out_shape=jax.ShapeDtypeStruct((NZ, a.shape[0], NC * rows), jnp.bfloat16),
        compiler_params=SCOPE,
        cost_estimate=pl.CostEstimate(
            flops=2 * a.size * NZ * NC * rows,
            bytes_accessed=2 * (a.size + NZ * NC * rows * (a.shape[0] + a.shape[1])),
            transcendentals=0,
        ),
    )(place, a, *own, *partners)


def body(step_states, norm_gain, w_qkv, w_out, prefix_cache, ancestors, prefix_lengths):
    t = lax.axis_index("tensor")
    y, xh = t // NXH, t % NXH
    z, c = lax.axis_index("particle") // NC, lax.axis_index("particle") % NC
    group_heads = Q_HEADS // KV_HEADS
    x0 = step_states[0]
    tokens, features = x0.shape
    shards = NY * NXH
    rows = w_out.shape[2] // 2

    w_full = lax.all_gather(w_qkv[0, 0], "particle", axis=0, tiled=True)

    pair = jnp.stack([x0, send(x0, dxh=1)])
    from_before = send(pair, dy=1)
    from_after = send(pair, dy=-1)
    far_a = send(from_before[0], dy=1)
    far_b = send(from_after[1], dy=-1)
    found = jnp.concatenate([pair, from_after, jnp.stack([far_a, far_b]), from_before], axis=0)
    blocks = [
        lax.dynamic_index_in_dim(
            found, ((k // NXH - y) % NY) * NXH + (k + xh) % NXH, axis=0, keepdims=False
        )
        for k in range(shards)
    ]
    full_rows = jnp.concatenate(blocks, axis=1).astype(jnp.float32)
    normed = (
        full_rows
        * lax.rsqrt(jnp.mean(full_rows * full_rows, -1, keepdims=True) + NORM_EPSILON)
        * norm_gain[0, 0]
    ).astype(jnp.bfloat16)

    hidden = send(x0, ds=1)
    picked, lengths = picked_cache(prefix_cache, ancestors, prefix_lengths)

    around = ring(w_out[0, 0, :rows])
    order = (0, 1, 7, 2, 6, 3, 5, 4)
    own = [around[k] for k in order]
    partners = [send(jnp.stack(own[:5]), dc=1), send(jnp.stack(own[5:]), dc=1)]

    cosine_part, sine_part = rotation(lengths, tokens // ancestors.shape[1], picked.shape[-1])
    cache = picked.reshape(picked.shape[0], 2, picked.shape[3], picked.shape[4])
    w_full, normed, cache, cosine_part, sine_part, hidden, own, partners = lax.optimization_barrier(
        (w_full, normed, cache, cosine_part, sine_part, hidden, own, partners)
    )
    second = lax.all_gather(w_out[0, 0, rows:], "particle", axis=0, tiled=True)
    projected = jnp.dot(normed, w_full, preferred_element_type=jnp.float32)
    attended = attend(projected, cosine_part, sine_part, cache, lengths, group_heads)

    results = []
    for half in range(2):
        if half == 0:
            terms = ring_terms(attended, order, own, partners, jnp.stack([z, c]))
        else:
            terms = head_terms(attended, second)
        terms = terms.reshape(NY, NXH, tokens, NC * rows)
        mid = tokens // 2

        def low_high(dy):
            block = lax.dynamic_index_in_dim(terms, (y + dy) % NY, axis=0, keepdims=False)
            return block[:, :mid], block[:, mid:]

        far_up, far_down = low_high(2)
        far_up, far_down = send(far_up, dy=1), send(far_down, dy=-1)
        up_low, up_high = low_high(1)
        down_low, down_high = low_high(-1)
        relay_up = (up_low.astype(jnp.float32) + far_up.astype(jnp.float32)).astype(jnp.bfloat16)
        relay_down = (down_high.astype(jnp.float32) + far_down.astype(jnp.float32)).astype(
            jnp.bfloat16
        )
        if half == 0:
            direct_up, direct_down = send(up_high, dy=1), send(down_low, dy=-1)
            from_below = jnp.concatenate([send(relay_up, dy=1), direct_up], axis=1)
            from_above = jnp.concatenate([direct_down, send(relay_down, dy=-1)], axis=1)
        else:
            from_below = send(jnp.concatenate([relay_up, up_high], axis=1), dy=1)
            from_above = send(jnp.concatenate([down_low, relay_down], axis=1), dy=-1)
        here_low, here_high = low_high(0)
        summed = (
            jnp.concatenate([here_low, here_high], axis=1).astype(jnp.float32)
            + from_below.astype(jnp.float32)
            + from_above.astype(jnp.float32)
        ).astype(jnp.bfloat16)
        same = send(jnp.where(xh == 0, summed[0], summed[1]), ds=1)
        cross = send(jnp.where(xh == 0, summed[1], summed[0]), ds=1, dxh=1)
        attended, same, cross = lax.optimization_barrier((attended, same, cross))
        results.append(same.astype(jnp.float32) + cross.astype(jnp.float32))
    summed = jnp.concatenate(
        [r[:, k * rows : (k + 1) * rows] for k in range(NC) for r in results], axis=1
    )
    return (hidden.astype(jnp.float32) + summed).astype(jnp.bfloat16)[None]


def solution(mesh):
    placed = (
        P("segment", "particle", "tensor"),
        P("segment", None, None),
        P("segment", None, "particle", "tensor"),
        P("segment", None, "particle", "tensor"),
        P("segment", None, "particle", None, "tensor", None, None),
        P("segment", "particle"),
        P("segment", None),
    )
    return jax.shard_map(
        body,
        mesh=mesh,
        in_specs=placed,
        out_specs=P("segment", "particle", "tensor"),
        check_vma=False,
    )
```

```python
import jax
import jax.numpy as jnp
from jax import lax
from jax.experimental import pallas as pl
from jax.experimental.pallas import tpu as pltpu
from jax.sharding import PartitionSpec as P

Q_HEADS = 32
KV_HEADS = 8

ROPE_BASE = 1000000.0
NORM_EPSILON = 1e-06

AXES = ("segment", "tensor", "particle")
SEG, NY, NXH, NZ, NC = 2, 4, 2, 8, 2
WIDE = 256
SCOPE = pltpu.CompilerParams(vmem_limit_bytes=40 * 2**20)


def moves(ds=0, dy=0, dxh=0, dz=0, dc=0):
    pairs = []
    for s in range(SEG):
        for y in range(NY):
            for xh in range(NXH):
                for z in range(NZ):
                    for c in range(NC):
                        src = ((s * NY + y) * NXH + xh) * NZ * NC + z * NC + c
                        to = (
                            ((s + ds) % SEG * NY + (y + dy) % NY) * NXH + (xh + dxh) % NXH
                        ) * NZ * NC + (z + dz) % NZ * NC + (c + dc) % NC
                        pairs.append((src, to))
    return pairs


def send(value, **shift):
    return lax.ppermute(value, AXES, moves(**shift))


def rotation(lengths, step_tokens, head_size):
    half_width = head_size // 2
    frequency = ROPE_BASE ** (
        -(jnp.arange(half_width, dtype=jnp.float32) * 2.0 / head_size)
    )
    positions = lengths[:, None] + jnp.arange(step_tokens, dtype=jnp.int32)[None, :]
    angles = positions.reshape(-1).astype(jnp.float32)[:, None] * frequency
    cosine_part = jnp.cos(angles)
    sine_part = jnp.sin(angles)
    return (
        jnp.concatenate([cosine_part, cosine_part], axis=1),
        jnp.concatenate([-sine_part, sine_part], axis=1),
    )


def attend_kernel(group_heads, lengths_ref, x_ref, cos_ref, sin_ref, cache_ref, o_ref):
    particles, _, prefix, head = cache_ref.shape
    steps = x_ref.shape[0] // particles
    score_scale = 1.0 / jnp.sqrt(jnp.float32(head))
    across = (((1,), (1,)), ((), ()))
    for p in range(particles):
        mine = pl.ds(p * steps, steps)
        cosine_part, sine_part = cos_ref[mine, :], sin_ref[mine, :]

        def rotated(k):
            v = x_ref[mine, k * head : (k + 1) * head]
            return v * cosine_part + pltpu.roll(v, head // 2, 1) * sine_part

        queries = jnp.concatenate([rotated(k) for k in range(group_heads)], axis=0)
        queries = queries.astype(jnp.bfloat16)
        keys_new = rotated(group_heads).astype(jnp.bfloat16)
        values_new = x_ref[mine, (group_heads + 1) * head :].astype(jnp.bfloat16)
        cache_scores = (
            lax.dot_general(queries, cache_ref[p, 0], across, preferred_element_type=jnp.float32)
            * score_scale
        )
        spots = lax.broadcasted_iota(jnp.int32, cache_scores.shape, 1)
        cache_scores = jnp.where(spots < lengths_ref[p], cache_scores, -1e30)
        step_scores = (
            lax.dot_general(queries, keys_new, across, preferred_element_type=jnp.float32)
            * score_scale
        )
        token = lax.rem(lax.broadcasted_iota(jnp.int32, step_scores.shape, 0), steps)
        other = lax.broadcasted_iota(jnp.int32, step_scores.shape, 1)
        step_scores = jnp.where(token >= other, step_scores, -1e30)
        peak = jnp.maximum(
            jnp.max(cache_scores, -1, keepdims=True), jnp.max(step_scores, -1, keepdims=True)
        )
        cache_weights = jnp.exp(cache_scores - peak)
        step_weights = jnp.exp(step_scores - peak)
        share = 1.0 / (
            jnp.sum(cache_weights, -1, keepdims=True) + jnp.sum(step_weights, -1, keepdims=True)
        )
        attended = jnp.dot(
            (cache_weights * share).astype(jnp.bfloat16),
            cache_ref[p, 1],
            preferred_element_type=jnp.float32,
        ) + jnp.dot(
            (step_weights * share).astype(jnp.bfloat16),
            values_new,
            preferred_element_type=jnp.float32,
        )
        attended = attended.astype(jnp.bfloat16)
        for k in range(group_heads):
            o_ref[mine, k * head : (k + 1) * head] = attended[k * steps : (k + 1) * steps]


def attend(projected, cosine_part, sine_part, cache, lengths, group_heads):
    head = cache.shape[-1]
    whole = pl.BlockSpec(memory_space=pltpu.VMEM)
    return pl.pallas_call(
        lambda *refs: attend_kernel(group_heads, *refs),
        in_specs=[pl.BlockSpec(memory_space=pltpu.SMEM)] + [whole] * 4,
        out_specs=whole,
        out_shape=jax.ShapeDtypeStruct((projected.shape[0], group_heads * head), jnp.bfloat16),
        compiler_params=SCOPE,
        cost_estimate=pl.CostEstimate(
            flops=4 * projected.shape[0] * group_heads * head * (cache.shape[2] + 64),
            bytes_accessed=2 * cache.size + 4 * projected.size,
            transcendentals=0,
        ),
    )(lengths, projected, cosine_part, sine_part, cache)


def one_hot(chosen, columns):
    return (chosen[:, None] == jnp.arange(columns, dtype=jnp.int32)[None, :]).astype(jnp.bfloat16)


def pick_rows(selector, source):
    flattened = source.reshape(source.shape[0], source.shape[1], -1)
    selected = jnp.einsum("jk,lkr->ljr", selector, flattened, preferred_element_type=jnp.float32)
    return selected.astype(jnp.bfloat16).reshape(
        (source.shape[0], selector.shape[0]) + source.shape[2:]
    )


def picked_cache(prefix_cache, ancestors, prefix_lengths):
    devices = lax.axis_size("particle")
    own_index = lax.axis_index("particle")
    per_device = ancestors.shape[1]
    parents = ancestors[0]
    length_table = prefix_lengths[0]
    lengths = jnp.sum(
        jnp.where(
            parents[:, None] == jnp.arange(length_table.shape[0], dtype=jnp.int32)[None, :],
            length_table[None, :],
            0,
        ),
        axis=1,
    )
    distance = (parents // per_device - own_index) % devices
    offset = jnp.where(distance == 0, 0, jnp.where(distance == 1, 1, -1))
    source_row = parents % per_device
    caches = prefix_cache[0]
    before = lax.ppermute(caches, "particle", [(i, (i + 1) % devices) for i in range(devices)])
    after = lax.ppermute(caches, "particle", [((i + 1) % devices, i) for i in range(devices)])
    extended = jnp.concatenate([before, caches, after], axis=1)
    picked = pick_rows(one_hot((offset + 1) * per_device + source_row, 3 * per_device), extended)
    return picked[0], lengths


def ring(block):
    half = block.shape[0] // 2
    found = {0: block}
    flow = {1: block, -1: block}
    for step in range(1, NZ // 2):
        for d in (1, -1):
            flow[d] = send(flow[d], dz=d)
            found[-d * step % NZ] = flow[d]
    far_low = send(flow[1][:half], dz=1)
    far_high = send(flow[-1][half:], dz=-1)
    found[NZ // 2] = jnp.concatenate([far_low, far_high], axis=0)
    return found


def term(a, w):
    return lax.dot_general(
        a, w, (((1,), (1,)), ((), ())), preferred_element_type=jnp.float32
    ).astype(jnp.bfloat16)


def terms_kernel(a_ref, w_ref, o_ref):
    o_ref[0] = term(a_ref[...], w_ref[...])


def head_terms(a, w):
    shards = NY * NXH
    rows = w.shape[0] // shards
    return pl.pallas_call(
        terms_kernel,
        grid=(shards,),
        in_specs=[
            pl.BlockSpec(a.shape, lambda k: (0, 0)),
            pl.BlockSpec((rows, w.shape[1]), lambda k: (k, 0)),
        ],
        out_specs=pl.BlockSpec((1, a.shape[0], rows), lambda k: (k, 0, 0)),
        out_shape=jax.ShapeDtypeStruct((shards, a.shape[0], rows), jnp.bfloat16),
        compiler_params=SCOPE,
        cost_estimate=pl.CostEstimate(
            flops=2 * a.size * w.shape[0],
            bytes_accessed=2 * (a.size + w.size + a.shape[0] * w.shape[0]),
            transcendentals=0,
        ),
    )(a, w)


def ring_terms_kernel(order, place_ref, a_ref, *refs):
    own, partners, o_ref = refs[: len(order)], refs[len(order) : -1], refs[-1]
    z, c = place_ref[0], place_ref[1]
    a = a_ref[...]
    others = [group.at[g] for group in partners for g in range(group.shape[0])]
    for k, block, other in zip(order, own, others):
        to = lax.rem(z + k, NZ)
        mine, theirs = term(a, block[...]), term(a, other[...])
        o_ref[to, :, pl.ds(pl.multiple_of(c * WIDE, WIDE), WIDE)] = mine[:, :WIDE]
        o_ref[to, :, pl.ds(pl.multiple_of((1 - c) * WIDE, WIDE), WIDE)] = theirs[:, :WIDE]
        mine, theirs = mine[:, WIDE:], theirs[:, WIDE:]
        o_ref[to, :, NC * WIDE :] = jnp.where(
            c == 0,
            jnp.concatenate([mine, theirs], axis=1),
            jnp.concatenate([theirs, mine], axis=1),
        )


def ring_terms(a, order, own, partners, place):
    rows = own[0].shape[0]
    whole = pl.BlockSpec(memory_space=pltpu.VMEM)
    return pl.pallas_call(
        lambda *refs: ring_terms_kernel(order, *refs),
        in_specs=[pl.BlockSpec(memory_space=pltpu.SMEM)]
        + [whole] * (1 + len(own) + len(partners)),
        out_specs=whole,
        out_shape=jax.ShapeDtypeStruct((NZ, a.shape[0], NC * rows), jnp.bfloat16),
        compiler_params=SCOPE,
        cost_estimate=pl.CostEstimate(
            flops=2 * a.size * NZ * NC * rows,
            bytes_accessed=2 * (a.size + NZ * NC * rows * (a.shape[0] + a.shape[1])),
            transcendentals=0,
        ),
    )(place, a, *own, *partners)


def body(step_states, norm_gain, w_qkv, w_out, prefix_cache, ancestors, prefix_lengths):
    t = lax.axis_index("tensor")
    y, xh = t // NXH, t % NXH
    z, c = lax.axis_index("particle") // NC, lax.axis_index("particle") % NC
    group_heads = Q_HEADS // KV_HEADS
    x0 = step_states[0]
    tokens, features = x0.shape
    shards = NY * NXH
    cut = w_out.shape[2] * 5 // 8

    w_full = lax.all_gather(w_qkv[0, 0], "particle", axis=0, tiled=True)

    pair = jnp.stack([x0, send(x0, dxh=1)])
    from_before = send(pair, dy=1)
    from_after = send(pair, dy=-1)
    far_a = send(from_before[0], dy=1)
    far_b = send(from_after[1], dy=-1)
    found = jnp.concatenate([pair, from_after, jnp.stack([far_a, far_b]), from_before], axis=0)
    blocks = [
        lax.dynamic_index_in_dim(
            found, ((k // NXH - y) % NY) * NXH + (k + xh) % NXH, axis=0, keepdims=False
        )
        for k in range(shards)
    ]
    full_rows = jnp.concatenate(blocks, axis=1).astype(jnp.float32)
    normed = (
        full_rows
        * lax.rsqrt(jnp.mean(full_rows * full_rows, -1, keepdims=True) + NORM_EPSILON)
        * norm_gain[0, 0]
    ).astype(jnp.bfloat16)

    hidden = send(x0, ds=1)
    picked, lengths = picked_cache(prefix_cache, ancestors, prefix_lengths)

    around = ring(w_out[0, 0, :cut])
    order = (0, 1, 7, 2, 6, 3, 5, 4)
    own = [around[k] for k in order]
    partners = [send(jnp.stack(own[:5]), dc=1), send(jnp.stack(own[5:]), dc=1)]

    cosine_part, sine_part = rotation(lengths, tokens // ancestors.shape[1], picked.shape[-1])
    cache = picked.reshape(picked.shape[0], 2, picked.shape[3], picked.shape[4])
    w_full, normed, cache, cosine_part, sine_part, hidden, own, partners = lax.optimization_barrier(
        (w_full, normed, cache, cosine_part, sine_part, hidden, own, partners)
    )
    second = lax.all_gather(w_out[0, 0, cut:], "particle", axis=0, tiled=True)
    projected = jnp.dot(normed, w_full, preferred_element_type=jnp.float32)
    attended = attend(projected, cosine_part, sine_part, cache, lengths, group_heads)

    results = []
    for half in range(2):
        if half == 0:
            terms = ring_terms(attended, order, own, partners, jnp.stack([z, c]))
        else:
            terms = head_terms(attended, second)
        terms = terms.reshape((NY, NXH) + terms.shape[1:])
        mid = tokens // 2

        def low_high(dy):
            block = lax.dynamic_index_in_dim(terms, (y + dy) % NY, axis=0, keepdims=False)
            return block[:, :mid], block[:, mid:]

        far_up, far_down = low_high(2)
        far_up, far_down = send(far_up, dy=1), send(far_down, dy=-1)
        up_low, up_high = low_high(1)
        down_low, down_high = low_high(-1)
        relay_up = (up_low.astype(jnp.float32) + far_up.astype(jnp.float32)).astype(jnp.bfloat16)
        relay_down = (down_high.astype(jnp.float32) + far_down.astype(jnp.float32)).astype(
            jnp.bfloat16
        )
        if half == 0:
            direct_up, direct_down = send(up_high, dy=1), send(down_low, dy=-1)
            from_below = jnp.concatenate([send(relay_up, dy=1), direct_up], axis=1)
            from_above = jnp.concatenate([direct_down, send(relay_down, dy=-1)], axis=1)
        else:
            from_below = send(jnp.concatenate([relay_up, up_high], axis=1), dy=1)
            from_above = send(jnp.concatenate([down_low, relay_down], axis=1), dy=-1)
        here_low, here_high = low_high(0)
        summed = (
            jnp.concatenate([here_low, here_high], axis=1).astype(jnp.float32)
            + from_below.astype(jnp.float32)
            + from_above.astype(jnp.float32)
        ).astype(jnp.bfloat16)
        attended, summed = lax.optimization_barrier((attended, summed))
        same = send(jnp.where(xh == 0, summed[0], summed[1]), ds=1)
        cross = send(jnp.where(xh == 0, summed[1], summed[0]), ds=1, dxh=1)
        results.append(same.astype(jnp.float32) + cross.astype(jnp.float32))
    early, late = results
    spare, tail = cut - WIDE, late.shape[1] // NC
    parts = []
    for k in range(NC):
        parts += [
            early[:, k * WIDE : (k + 1) * WIDE],
            early[:, NC * WIDE + k * spare : NC * WIDE + (k + 1) * spare],
            late[:, k * tail : (k + 1) * tail],
        ]
    summed = jnp.concatenate(parts, axis=1)
    return (hidden.astype(jnp.float32) + summed).astype(jnp.bfloat16)[None]


def solution(mesh):
    placed = (
        P("segment", "particle", "tensor"),
        P("segment", None, None),
        P("segment", None, "particle", "tensor"),
        P("segment", None, "particle", "tensor"),
        P("segment", None, "particle", None, "tensor", None, None),
        P("segment", "particle"),
        P("segment", None),
    )
    return jax.shard_map(
        body,
        mesh=mesh,
        in_specs=placed,
        out_specs=P("segment", "particle", "tensor"),
        check_vma=False,
    )
```
